32 devices in a mesh: dp: 8 (over z, x), bank: 4 (over y, core).
Axes of the slice: x: 2, y: 2, z: 4, core: 2. Of those that a mesh axis runs over, the one named last changes fastest.
Arguments:
- features: float32 [128, 128], P('dp'), may hold values from -6 to 6
- video_ids: int32 [8, 16], P('dp'), may hold values from 0 to 4, never falling along the last dimension, each value on 1 to 8 neighbouring positions
- bank: float32 [16384, 128], P(('dp', 'bank')), may hold values from -6 to 6
- loss_weight: float32 [128], P('dp'), may hold values from 0.5 to 2
Outputs:
- loss: float32 [128], P('dp')
- feature_grad: float32 [128, 128], P('dp')
The draws below stay inside these ranges and needn't reach their ends.
Inputs may be any that keep to these rules, and one draw needn't show every extreme that they name: `video_ids`: each row of 16 frames holds 5 videos as runs of equal ids in ascending order, each video 1 to 8 frames and one exactly 8.
All inputs are finite; a program needn't handle non-finite values.
Results may differ from the reference program's by a relative error of at most 0.0003.
Values sent between devices are 32-bit elements; how exact they have to be, the bound alone decides.
A program may use at most 64 MiB of HBM per device.

```python
import math
import jax
import jax.numpy as jnp
import numpy as np
from jax import lax

FEAT = 128
Q_DEV = 16
VIDS = 5
MAXLEN = 8
QUERIES = 128
BANK = 16384
N_DP = 8


def block_levels(own_key, dims, cuts, least, top_value):
    gain = 1.0
    for dim, shards_of in cuts:
        steps = jax.random.uniform(jax.random.fold_in(jax.random.fold_in(own_key, 6), dim), (shards_of,), jnp.float32, least / len(cuts), top_value / len(cuts))
        gain = gain * jnp.repeat(jnp.exp(steps), dims[dim] // shards_of).reshape((-1,) + (1,) * (len(dims) - 1 - dim))
    return gain


def length_profile(amount, total, bound, slope):
    weights = [(1 << 20) // math.isqrt(grade ** slope) + 1 for grade in range(2, amount + 1)]
    rest, counts = total - bound - (amount - 1), [1] * (amount - 1)
    while rest > 0:
        movable = [i for i in range(amount - 1) if counts[i] < bound]
        whole, remaining = sum([weights[i] for i in movable]), rest
        for i in movable:
            addition = min(bound - counts[i], max(1, remaining * weights[i] // whole), rest)
            counts[i] = counts[i] + addition
            rest = rest - addition
    return np.array([bound] + counts)


def ragged(own_key, count, total, reach, lean):
    if count == 2:
        one = jax.random.randint(own_key, (), max(1, total - reach), min(reach, total - 1) + 1)
        return jnp.stack([one, total - one])
    sizes = jnp.asarray(length_profile(count, total, reach, lean), jnp.int32)
    pairs = (count - 1) // 2
    source_of, sink = sizes[1:1 + 2 * pairs:2], sizes[2:2 + 2 * pairs:2]
    margin = jnp.minimum(source_of - 1, reach - sink)
    moved = jax.random.randint(jax.random.fold_in(own_key, 1), (pairs,), 0, 1 << 20) % (margin + 1)
    sizes = sizes.at[1:1 + 2 * pairs:2].set(source_of - moved).at[2:2 + 2 * pairs:2].set(sink + moved)
    return sizes[jax.random.permutation(jax.random.fold_in(own_key, 2), count)]


def gaussian(stream_key, extent, width, limit, split=(), kind=jnp.bfloat16):
    values = width * jax.random.normal(stream_key, extent, jnp.float32)
    if split:
        values = values * block_levels(stream_key, extent, split, -0.22, 0.18)
    return jnp.clip(values, -limit, limit).astype(kind)


def setup_inputs(seed: int = 0) -> dict:
    seeds = jax.random.split(jax.random.key(seed), 5)
    return {
        "features": gaussian(seeds[0], (QUERIES, FEAT), 1.0, 6.0, ((0, 8),), jnp.float32),
        "video_ids": jax.vmap(lambda own: jnp.searchsorted(jnp.cumsum(ragged(own, VIDS, Q_DEV, MAXLEN, 2)), jnp.arange(Q_DEV), side="right"))(jax.random.split(seeds[1], N_DP)).reshape((N_DP, Q_DEV)).astype(jnp.int32),
        "bank": gaussian(seeds[2], (BANK, FEAT), 1.0, 6.0, ((0, 32),), jnp.float32),
        "loss_weight": jnp.clip(0.5 + 1.5 * jax.random.uniform(seeds[3], (QUERIES,), jnp.float32) ** block_levels(seeds[3], (QUERIES,), ((0, 8),), -0.2, 0.2), 0.5, 2.0),
    }


EPSILON = 1e-06
TAU_BACK = 0.1
HIGHEST = lax.Precision.HIGHEST

def unit_rows(values):
    return values / jnp.sqrt(lax.optimization_barrier(jnp.sum(values * values, axis=1, keepdims=True)) + EPSILON)

def cycle_loss(neighbour, normed, videos):
    frames = videos.shape[0]
    same_video = videos[:, None] == videos[None, :]
    row_index = lax.broadcasted_iota(jnp.int32, (frames, frames), 0)
    col_index = lax.broadcasted_iota(jnp.int32, (frames, frames), 1)
    earlier = same_video & (col_index < row_index)
    position = lax.optimization_barrier(jnp.sum(jnp.where(earlier, 1.0, 0.0), axis=1)).astype(neighbour.dtype)
    products = jnp.dot(neighbour, normed.T, precision=HIGHEST)
    distance = lax.optimization_barrier(jnp.sum(neighbour * neighbour, axis=1))[:, None] - 2.0 * products + lax.optimization_barrier(jnp.sum(normed * normed, axis=1))[None, :]
    back_weight = jnp.where(same_video, jnp.exp(-distance / TAU_BACK), 0.0).astype(neighbour.dtype)
    back_weight = back_weight / lax.optimization_barrier(jnp.sum(back_weight, axis=1, keepdims=True))
    mean_pos = jnp.dot(back_weight, position, precision=HIGHEST)
    square_pos = jnp.dot(back_weight, position * position, precision=HIGHEST)
    spread = jnp.maximum(square_pos - mean_pos * mean_pos, 1.0)
    return (position - mean_pos) ** 2 / spread + 0.5 * jnp.log(spread)

def reference(features, video_ids, bank, loss_weight):
    sharpness = 3.0 * math.sqrt(FEAT)
    lengths = jnp.sqrt(lax.optimization_barrier(jnp.sum(features * features, axis=1, keepdims=True)) + EPSILON)
    normed = features / lengths
    keys = unit_rows(bank)
    rows_block = math.gcd(keys.shape[0], 8192)
    key_blocks = keys.reshape(-1, rows_block, FEAT)

    def forward_block(running, key_block):
        exp_scores = jnp.exp(sharpness * jnp.dot(normed, key_block.T, precision=HIGHEST))
        summed = running[0] + jnp.dot(exp_scores, key_block, precision=HIGHEST)
        return ((summed, running[1] + lax.optimization_barrier(jnp.sum(exp_scores, axis=1))), None)
    start_carry = (jnp.zeros(normed.shape, features.dtype), jnp.zeros((normed.shape[0],), features.dtype))
    (summed, partition), _ = lax.scan(forward_block, start_carry, key_blocks)
    neighbour = summed / partition[:, None]

    def cycle_part(soft_rows, unit_part):
        losses = jax.vmap(cycle_loss)(soft_rows.reshape(-1, Q_DEV, FEAT), unit_part.reshape(-1, Q_DEV, FEAT), video_ids)
        return losses.reshape(-1)
    loss, pullback = jax.vjp(cycle_part, neighbour, normed)
    grad_soft, grad_local = pullback(loss_weight)

    def backward_block(running, key_block):
        exp_scores = jnp.exp(sharpness * jnp.dot(normed, key_block.T, precision=HIGHEST))
        projected = jnp.dot(grad_soft, key_block.T, precision=HIGHEST)
        return (running + jnp.dot(exp_scores * projected, key_block, precision=HIGHEST), None)
    moment, _ = lax.scan(backward_block, jnp.zeros(normed.shape, features.dtype), key_blocks)
    along = lax.optimization_barrier(jnp.sum(grad_soft * neighbour, axis=1, keepdims=True))
    grad_unit = grad_local + sharpness * (moment / partition[:, None] - along * neighbour)
    feature_grad = (grad_unit - normed * lax.optimization_barrier(jnp.sum(normed * grad_unit, axis=1, keepdims=True))) / lengths
    return (loss, feature_grad)
```

```python
import functools
import math

import jax
import jax.numpy as jnp
from jax import lax
from jax.experimental import pallas as pl
from jax.experimental.pallas import tpu as pltpu
from jax.sharding import PartitionSpec as P

EPSILON = 1e-06
TAU_BACK = 0.1
HIGHEST = lax.Precision.HIGHEST
MESH = pl.DeviceIdType.MESH
F32, BF16 = jnp.float32, jnp.bfloat16
TILE = 8
NT = (((1,), (1,)), ((), ()))
TN = (((0,), (0,)), ((), ()))
NN = (((1,), (0,)), ((), ()))


def split(values):
    high = values.astype(BF16)
    low = (values - high.astype(F32)).astype(BF16)
    return high, low


def inverse_lengths(values):
    return lax.rsqrt(jnp.sum(values * values, axis=1, keepdims=True) + EPSILON)


def cycle(near, normed, squares, same, pos_row, pos_col, weight):
    products = lax.dot_general(near, normed, NT, precision=HIGHEST, preferred_element_type=F32)
    distance = jnp.sum(near * near, axis=1, keepdims=True) - 2.0 * products + squares
    back = jnp.where(same, jnp.exp(-distance / TAU_BACK), 0.0)
    beta = back / jnp.sum(back, axis=1, keepdims=True)
    mean = jnp.sum(beta * pos_row, axis=1, keepdims=True)
    square = jnp.sum(beta * (pos_row * pos_row), axis=1, keepdims=True)
    variance = square - mean * mean
    spread = jnp.maximum(variance, 1.0)
    off = pos_col - mean
    loss = off * off / spread + 0.5 * jnp.log(spread)
    d_spread = 0.5 / spread - off * off / (spread * spread)
    slope = jnp.where(variance > 1.0, 1.0, jnp.where(variance == 1.0, 0.5, 0.0))
    d_square = d_spread * slope
    d_mean = -2.0 * off / spread - 2.0 * mean * d_square
    d_beta = d_mean * pos_row + d_square * (pos_row * pos_row)
    d_logit = beta * (d_beta - (d_mean * mean + d_square * square))
    return loss, d_logit * weight * (-1.0 / TAU_BACK)


def kernel(
    owners, banks, sharpness,
    feat_ref, ids_ref, bank_ref, weight_ref,
    loss_ref, grad_ref,
    keys_buf, k3, kcat, raw, expo, send1, recv1, tile2, recv2, send3, recv3, tile4, recv4,
    bank_sem, send_sems, recv_sems,
):
    frames, width = feat_ref.shape
    share = frames // banks
    per_tile = TILE // share
    count = owners * banks
    block = min(owners * frames, 128)
    blocks = owners * frames // block
    tiles = block // TILE
    own = lax.axis_index("dp")
    part = lax.axis_index("bank")
    me = own * banks + part

    load = pltpu.make_async_copy(bank_ref, keys_buf, bank_sem)
    load.start()
    barrier = pltpu.get_barrier_semaphore()

    def everyone(body):
        def step(k, carry):
            dst = lax.rem(me + k, count)
            body(dst, (lax.div(dst, banks), lax.rem(dst, banks)))
            return carry
        lax.fori_loop(1, count, step, 0, unroll=count <= 32)

    everyone(lambda dst, where: pl.semaphore_signal(barrier, inc=1, device_id=where, device_id_type=MESH))

    features = feat_ref[...]
    inv_own = inverse_lengths(features)
    normed = features * inv_own
    ones = jnp.ones((TILE, width), F32)
    squares = lax.dot_general(ones, normed * normed, NT, precision=HIGHEST, preferred_element_type=F32)[0:1]
    ids = ids_ref[...].astype(F32)
    weights = weight_ref[...]

    def column(row, first, rows):
        pick = lax.broadcasted_iota(jnp.int32, (rows, frames), 1) == (
            lax.broadcasted_iota(jnp.int32, (rows, frames), 0) + first)
        return jnp.sum(jnp.where(pick, jnp.broadcast_to(row, (rows, frames)), 0.0), axis=1, keepdims=True)

    rows16 = lax.broadcasted_iota(jnp.int32, (frames, frames), 0)
    cols16 = lax.broadcasted_iota(jnp.int32, (frames, frames), 1)
    same_all = column(ids, 0, frames) == ids
    pos_row = jnp.sum(jnp.where(same_all & (rows16 < cols16), 1.0, 0.0), axis=0, keepdims=True)
    pos_all = column(pos_row, 0, frames)
    weight_all = column(weights, 0, frames)
    mine = part * share
    same_mine = column(ids, mine, share) == ids
    pos_mine = column(pos_row, mine, share)
    weight_mine = column(weights, mine, share)

    pl.semaphore_wait(barrier, count - 1)

    def send_features(k, carry):
        dst = lax.rem(own + k, owners)
        pltpu.make_async_remote_copy(
            src_ref=feat_ref, dst_ref=raw.at[own], send_sem=send_sems.at[0], recv_sem=recv_sems.at[0],
            device_id=(dst, part), device_id_type=MESH).start()
        return carry
    lax.fori_loop(1, owners, send_features, 0, unroll=owners <= 8)
    raw[own] = features

    load.wait()
    bank = keys_buf[...]
    key_high, key_low = split(bank * inverse_lengths(bank))
    k3[:, 0:width] = key_high
    k3[:, width:2 * width] = key_high
    k3[:, 2 * width:3 * width] = key_low
    kcat[:, 0:width] = key_high
    kcat[:, width:2 * width] = key_low

    def wait(ref, sem):
        pltpu.make_async_copy(ref, ref, sem).wait()

    wait(raw.at[pl.ds(0, owners - 1)], recv_sems.at[0])

    def project(values):
        high, low = split(values)
        joined = jnp.concatenate([high, low, high], axis=1)
        return lax.dot_general(joined, k3[...], NT, preferred_element_type=F32)

    def collect(values):
        high, low = split(values)
        both = lax.dot_general(high, kcat[...], NN, preferred_element_type=F32)
        rest = lax.dot_general(low, kcat[:, 0:width], NN, preferred_element_type=F32)
        return both[:, 0:width] + (both[:, width:2 * width] + rest)

    group = block // frames

    def forward(index, carry):
        queries = raw[pl.ds(index * group, group)].reshape(block, width)
        queries = queries * inverse_lengths(queries)
        scores = jnp.exp(sharpness * project(queries))
        expo[index] = scores
        summed = collect(scores)
        partition = jnp.broadcast_to(jnp.sum(scores, axis=1, keepdims=True), (block, width))
        base = index * (tiles * per_tile)
        for t in range(tiles * per_tile):
            send1[base + t, 0:share, :] = summed[t * share:(t + 1) * share]
            send1[base + t, share:2 * share, :] = partition[t * share:(t + 1) * share]
        return carry
    if blocks == 1:
        forward(0, 0)
    else:
        lax.fori_loop(0, blocks, forward, 0)

    def spread_out(slot, source, target):
        everyone(lambda dst, where: pltpu.make_async_remote_copy(
            src_ref=source(dst), dst_ref=target.at[me], send_sem=send_sems.at[slot], recv_sem=recv_sems.at[slot],
            device_id=where, device_id_type=MESH).start())

    spread_out(1, lambda dst: send1.at[dst], recv1)
    recv1[me] = send1[me]
    wait(recv1.at[pl.ds(0, count - 1)], recv_sems.at[1])
    total = jnp.sum(recv1[...], axis=0)
    inv_part = 1.0 / total[share:2 * share]
    near = total[0:share] * inv_part
    _, d_dist = cycle(near, normed, squares, same_mine, pos_row, pos_mine, weight_mine)
    grad_soft = 2.0 * (
        near * jnp.sum(d_dist, axis=1, keepdims=True)
        - lax.dot_general(d_dist, normed, NN, precision=HIGHEST, preferred_element_type=F32))

    tile2[...] = jnp.zeros_like(tile2)
    tile2[0:share, :] = grad_soft
    tile2[share:2 * share, :] = near
    spread_out(2, lambda dst: tile2, recv2)
    recv2[me] = tile2[...]
    along = jnp.sum(grad_soft * near, axis=1, keepdims=True)
    wait(recv2.at[pl.ds(0, count - 1)], recv_sems.at[2])

    def backward(index, carry):
        base = index * (tiles * per_tile)
        held = recv2[pl.ds(base, tiles * per_tile)]
        grads = jnp.concatenate([held[t, 0:share] for t in range(tiles * per_tile)], axis=0)
        moment = collect(expo[index] * project(grads))
        for t in range(tiles * per_tile):
            send3[base + t] = moment[t * share:(t + 1) * share]
        return carry
    if blocks == 1:
        backward(0, 0)
    else:
        lax.fori_loop(0, blocks, backward, 0)

    spread_out(3, lambda dst: send3.at[dst], recv3)
    recv3[me] = send3[me]

    first = own * banks
    group_rows = recv2[pl.ds(first, banks)]
    near_all = jnp.concatenate([group_rows[b, share:2 * share] for b in range(banks)], axis=0)
    loss, d_dist_all = cycle(near_all, normed, squares, same_all, pos_row, pos_all, weight_all)
    loss_ref[...] = jnp.sum(jnp.where(rows16 == cols16, jnp.broadcast_to(loss, (frames, frames)), 0.0), axis=0, keepdims=True)
    column_sums = lax.dot_general(d_dist_all, jnp.ones((frames, width), F32), TN, precision=HIGHEST, preferred_element_type=F32)
    grad_local = 2.0 * (
        normed * column_sums
        - lax.dot_general(d_dist_all, near_all, TN, precision=HIGHEST, preferred_element_type=F32))

    wait(recv3.at[pl.ds(0, count - 1)], recv_sems.at[3])
    moment = jnp.sum(recv3[...], axis=0)
    tile4[...] = sharpness * (moment * inv_part - along * near)

    for k in range(1, banks):
        pltpu.make_async_remote_copy(
            src_ref=tile4, dst_ref=recv4.at[part], send_sem=send_sems.at[4], recv_sem=recv_sems.at[4],
            device_id=(own, lax.rem(part + k, banks)), device_id_type=MESH).start()
    recv4[part] = tile4[...]
    wait(recv4.at[pl.ds(0, banks - 1)], recv_sems.at[4])
    held = recv4[...]
    grad_unit = grad_local + jnp.concatenate([held[b] for b in range(banks)], axis=0)
    grad_ref[...] = (grad_unit - normed * jnp.sum(normed * grad_unit, axis=1, keepdims=True)) * inv_own

    wait(raw.at[pl.ds(0, owners - 1)], send_sems.at[0])
    wait(recv1.at[pl.ds(0, count - 1)], send_sems.at[1])
    wait(recv2.at[pl.ds(0, count - 1)], send_sems.at[2])
    wait(recv3.at[pl.ds(0, count - 1)], send_sems.at[3])
    wait(recv4.at[pl.ds(0, banks - 1)], send_sems.at[4])


def shards(owners, banks, features, video_ids, bank, loss_weight):
    frames, width = features.shape
    keys = bank.shape[0]
    count = owners * banks
    share = frames // banks
    block = min(owners * frames, 128)
    blocks = owners * frames // block
    vmem = pl.BlockSpec(memory_space=pltpu.VMEM)
    loss, grad = pl.pallas_call(
        functools.partial(kernel, owners, banks, 3.0 * math.sqrt(width)),
        out_shape=(jax.ShapeDtypeStruct((1, frames), F32), jax.ShapeDtypeStruct((frames, width), F32)),
        in_specs=[vmem, vmem, pl.BlockSpec(memory_space=pl.ANY), vmem],
        out_specs=(vmem, vmem),
        scratch_shapes=[
            pltpu.VMEM((keys, width), F32),
            pltpu.VMEM((keys, 3 * width), BF16),
            pltpu.VMEM((keys, 2 * width), BF16),
            pltpu.VMEM((owners, frames, width), F32),
            pltpu.VMEM((blocks, block, keys), F32),
            pltpu.VMEM((count, TILE, width), F32),
            pltpu.VMEM((count, TILE, width), F32),
            pltpu.VMEM((TILE, width), F32),
            pltpu.VMEM((count, TILE, width), F32),
            pltpu.VMEM((count, share, width), F32),
            pltpu.VMEM((count, share, width), F32),
            pltpu.VMEM((share, width), F32),
            pltpu.VMEM((banks, share, width), F32),
            pltpu.SemaphoreType.DMA,
            pltpu.SemaphoreType.DMA((5,)),
            pltpu.SemaphoreType.DMA((5,)),
        ],
        compiler_params=pltpu.CompilerParams(
            collective_id=0, has_side_effects=True, vmem_limit_bytes=48 * 1024 * 1024),
    )(features, video_ids, bank, loss_weight.reshape(1, frames))
    return loss.reshape(frames), grad


def solution(mesh):
    return jax.shard_map(
        functools.partial(shards, mesh.shape["dp"], mesh.shape["bank"]),
        mesh=mesh,
        in_specs=(P("dp", None), P("dp", None), P(("dp", "bank"), None), P("dp")),
        out_specs=(P("dp"), P("dp", None)),
        check_vma=False,
    )
```

```python
import functools
import math

import jax
import jax.numpy as jnp
from jax import lax
from jax.experimental import pallas as pl
from jax.experimental.pallas import tpu as pltpu
from jax.sharding import PartitionSpec as P

EPSILON = 1e-06
TAU_BACK = 0.1
HIGHEST = lax.Precision.HIGHEST
MESH = pl.DeviceIdType.MESH
F32, BF16 = jnp.float32, jnp.bfloat16
TILE = 8
NT = (((1,), (1,)), ((), ()))
TN = (((0,), (0,)), ((), ()))
NN = (((1,), (0,)), ((), ()))


def split(values):
    high = values.astype(BF16)
    low = (values - high.astype(F32)).astype(BF16)
    return high, low


def inverse_lengths(values):
    return lax.rsqrt(jnp.sum(values * values, axis=1, keepdims=True) + EPSILON)


def cycle(near, normed, squares, same, pos_row, pos_col, weight):
    products = lax.dot_general(near, normed, NT, precision=HIGHEST, preferred_element_type=F32)
    norms = jnp.sum(near * near, axis=1, keepdims=True)
    distance = norms - 2.0 * products + squares
    back = jnp.where(same, jnp.exp(-distance / TAU_BACK), 0.0)
    beta = back / jnp.sum(back, axis=1, keepdims=True)
    mean = jnp.sum(beta * pos_row, axis=1, keepdims=True)
    square = jnp.sum(beta * (pos_row * pos_row), axis=1, keepdims=True)
    variance = square - mean * mean
    spread = jnp.maximum(variance, 1.0)
    off = pos_col - mean
    loss = off * off / spread + 0.5 * jnp.log(spread)
    d_spread = 0.5 / spread - off * off / (spread * spread)
    slope = jnp.where(variance > 1.0, 1.0, jnp.where(variance == 1.0, 0.5, 0.0))
    d_square = d_spread * slope
    d_mean = -2.0 * off / spread - 2.0 * mean * d_square
    d_beta = d_mean * pos_row + d_square * (pos_row * pos_row)
    d_logit = beta * (d_beta - (d_mean * mean + d_square * square))
    d_dist = d_logit * weight * (-1.0 / TAU_BACK)
    along = 2.0 * jnp.sum(d_dist * (norms - products), axis=1, keepdims=True)
    return loss, d_dist, along


def kernel(
    owners, banks, sharpness,
    feat_hbm, ids_hbm, bank_ref, weight_hbm,
    loss_ref, grad_ref,
    feat_ref, ids_ref, weight_ref, keys_buf, k3, kcat, out0, raw, score, expo,
    send1, recvx, recv1, tile4, recv4,
    load_sems, send_sems, recv_sems,
):
    frames, width = feat_hbm.shape
    share = frames // banks
    halves = banks // 2
    cells = owners * halves
    folds = frames // TILE
    block = min(owners * frames, 128)
    blocks = owners * frames // block
    group = block // frames
    own = lax.axis_index("dp")
    part = lax.axis_index("bank")
    side = lax.rem(part, 2)
    twin = part + 1 - 2 * side
    cell = own * halves + lax.div(part, 2)

    loads = [
        pltpu.make_async_copy(feat_hbm, feat_ref, load_sems.at[0]),
        pltpu.make_async_copy(bank_ref, keys_buf, load_sems.at[1]),
        pltpu.make_async_copy(ids_hbm, ids_ref, load_sems.at[2]),
        pltpu.make_async_copy(weight_hbm, weight_ref, load_sems.at[3]),
    ]
    for load in loads:
        load.start()
    barrier = pltpu.get_barrier_semaphore()

    def every_cell(body):
        def step(k, carry):
            dst = lax.rem(cell + k, cells)
            body(dst, (lax.div(dst, halves), 2 * lax.rem(dst, halves) + side))
            return carry
        lax.fori_loop(1, cells, step, 0, unroll=cells <= 16)

    every_cell(lambda dst, where: pl.semaphore_signal(barrier, inc=1, device_id=where, device_id_type=MESH))
    for k in range(1, banks, 2):
        pl.semaphore_signal(barrier, inc=1, device_id=(own, lax.rem(part + k, banks)), device_id_type=MESH)

    for index in (0, 2, 3):
        loads[index].wait()
    features = feat_ref[...]
    inv_own = inverse_lengths(features)
    normed = features * inv_own
    ones = jnp.ones((TILE, width), F32)
    squares = lax.dot_general(ones, normed * normed, NT, precision=HIGHEST, preferred_element_type=F32)[0:1]
    ids = ids_ref[...].astype(F32)
    weights = weight_ref[...]

    def column(row, first, rows):
        pick = lax.broadcasted_iota(jnp.int32, (rows, frames), 1) == (
            lax.broadcasted_iota(jnp.int32, (rows, frames), 0) + first)
        return jnp.sum(jnp.where(pick, jnp.broadcast_to(row, (rows, frames)), 0.0), axis=1, keepdims=True)

    rows16 = lax.broadcasted_iota(jnp.int32, (frames, frames), 0)
    cols16 = lax.broadcasted_iota(jnp.int32, (frames, frames), 1)
    same_all = column(ids, 0, frames) == ids
    pos_row = jnp.sum(jnp.where(same_all & (rows16 < cols16), 1.0, 0.0), axis=0, keepdims=True)
    mine = part * share
    same_mine = column(ids, mine, share) == ids
    pos_mine = column(pos_row, mine, share)
    weight_mine = column(weights, mine, share)

    out0[0:frames, :] = features
    out0[frames:2 * frames, :] = jnp.zeros((frames, width), F32)
    out0[frames:2 * frames, 0:frames] = jnp.where(same_all, 1.0, 0.0)

    pl.semaphore_wait(barrier, cells - 1 + halves)

    def send_features(k, carry):
        dst = lax.rem(own + k, owners)
        pltpu.make_async_remote_copy(
            src_ref=out0, dst_ref=raw.at[own], send_sem=send_sems.at[0], recv_sem=recv_sems.at[0],
            device_id=(dst, part), device_id_type=MESH).start()
        return carry
    lax.fori_loop(1, owners, send_features, 0, unroll=owners <= 8)
    raw[own] = out0[...]

    loads[1].wait()
    bank = keys_buf[...]
    key_high, key_low = split(bank * inverse_lengths(bank))
    k3[:, 0:width] = key_high
    k3[:, width:2 * width] = key_high
    k3[:, 2 * width:3 * width] = key_low
    kcat[:, 0:width] = key_high
    kcat[:, width:2 * width] = key_low

    def wait(ref, sem):
        pltpu.make_async_copy(ref, ref, sem).wait()

    def project(values):
        high, low = split(values)
        joined = jnp.concatenate([high, low, high], axis=1)
        return lax.dot_general(joined, k3[...], NT, preferred_element_type=F32)

    def collect(values):
        high, low = split(values)
        both = lax.dot_general(high, kcat[...], NN, preferred_element_type=F32)
        rest = lax.dot_general(low, kcat[:, 0:width], NN, preferred_element_type=F32)
        return both[:, 0:width] + (both[:, width:2 * width] + rest)

    def each(count, body):
        if count <= 8:
            for k in range(count):
                body(k)
        else:
            lax.fori_loop(0, count, lambda k, carry: (body(k), carry)[1], 0)

    wait(raw.at[pl.ds(0, owners - 1)], recv_sems.at[0])

    def forward(index):
        queries = raw[pl.ds(index * group, group), 0:frames].reshape(block, width)
        scores = project(queries * inverse_lengths(queries))
        weighted = jnp.exp(sharpness * scores)
        score[...] = scores
        expo[...] = weighted
        summed = collect(weighted)
        partition = jnp.broadcast_to(jnp.sum(weighted, axis=1, keepdims=True), (block, width))
        for g in range(group):
            owner = index * group + g
            shared = raw[owner, frames:2 * frames, 0:frames]
            for b in range(banks):
                spot = send1.at[b % 2, owner * halves + b // 2]
                row = g * frames + b * share
                spot[0:share, :] = summed[row:row + share]
                spot[share:2 * share, :] = partition[row:row + share]
            pairs = []
            for i in range(frames):
                picked = None
                for f in range(folds):
                    term = shared[f * TILE:(f + 1) * TILE, i:i + 1] * score[pl.ds(g * frames + f * TILE, TILE), :]
                    picked = term if picked is None else picked + term
                pairs.append(picked * expo[pl.ds(g * frames + i, 1), :])
            second = collect(jnp.concatenate(pairs, axis=0))
            for i in range(frames):
                b = i // share
                first = TILE + (i % share) * TILE
                send1[b % 2, owner * halves + b // 2, first:first + TILE, :] = second[i * TILE:(i + 1) * TILE]
    each(blocks, forward)

    pltpu.make_async_remote_copy(
        src_ref=send1.at[1 - side], dst_ref=recvx, send_sem=send_sems.at[1], recv_sem=recv_sems.at[1],
        device_id=(own, twin), device_id_type=MESH).start()
    wait(recvx, recv_sems.at[1])
    send1[side] = send1[side] + recvx[...]

    every_cell(lambda dst, where: pltpu.make_async_remote_copy(
        src_ref=send1.at[side, dst], dst_ref=recv1.at[cell], send_sem=send_sems.at[2], recv_sem=recv_sems.at[2],
        device_id=where, device_id_type=MESH).start())
    recv1[cell] = send1[side, cell]
    wait(recv1.at[pl.ds(0, cells - 1)], recv_sems.at[2])
    total = jnp.sum(recv1[...], axis=0)
    inv_part = 1.0 / total[share:2 * share]
    near = total[0:share] * inv_part
    loss, d_dist, along = cycle(near, normed, squares, same_mine, pos_row, pos_mine, weight_mine)
    pairs = share * TILE
    fold = jnp.where(
        lax.rem(lax.broadcasted_iota(jnp.int32, (frames, pairs), 0), TILE)
        == lax.rem(lax.broadcasted_iota(jnp.int32, (frames, pairs), 1), TILE), -2.0, 0.0)
    factors = lax.dot_general(d_dist, fold, NN, precision=HIGHEST, preferred_element_type=F32)
    factors = jnp.where(
        lax.div(lax.broadcasted_iota(jnp.int32, (share, pairs), 1), TILE)
        == lax.broadcasted_iota(jnp.int32, (share, pairs), 0), factors, 0.0)
    moment = lax.dot_general(factors, total[TILE:TILE + pairs], NN, precision=HIGHEST, preferred_element_type=F32)
    rows = sharpness * (moment * inv_part - along * near)
    joined = jnp.concatenate([near, jnp.ones((share, width), F32)], axis=1)
    local = lax.dot_general(d_dist, joined, TN, precision=HIGHEST, preferred_element_type=F32)
    local = 2.0 * (normed * local[:, width:2 * width] - local[:, 0:width])
    placed = jnp.concatenate([rows] * banks, axis=0)
    is_mine = lax.div(lax.broadcasted_iota(jnp.int32, (frames, width), 0), share) == part
    tile4[0:frames, :] = local + jnp.where(is_mine, placed, 0.0)
    tile4[frames:frames + TILE, :] = jnp.zeros((TILE, width), F32)
    tile4[frames:frames + share, :] = jnp.broadcast_to(loss, (share, width))

    for k in range(1, banks):
        pltpu.make_async_remote_copy(
            src_ref=tile4, dst_ref=recv4.at[part], send_sem=send_sems.at[3], recv_sem=recv_sems.at[3],
            device_id=(own, lax.rem(part + k, banks)), device_id_type=MESH).start()
    recv4[part] = tile4[...]
    wait(raw.at[pl.ds(0, owners - 1)], send_sems.at[0])
    wait(recvx, send_sems.at[1])
    wait(recv1.at[pl.ds(0, cells - 1)], send_sems.at[2])
    wait(recv4.at[pl.ds(0, banks - 1)], recv_sems.at[3])
    held = recv4[...]
    grad_unit = jnp.sum(held[:, 0:frames], axis=0)
    grad_ref[...] = (grad_unit - normed * jnp.sum(normed * grad_unit, axis=1, keepdims=True)) * inv_own
    losses = jnp.concatenate([held[b, frames:frames + share] for b in range(banks)], axis=0)[:, 0:frames]
    loss_ref[...] = jnp.sum(jnp.where(rows16 == cols16, losses, 0.0), axis=0, keepdims=True)
    wait(recv4.at[pl.ds(0, banks - 1)], send_sems.at[3])


def shards(owners, banks, features, video_ids, bank, loss_weight):
    frames, width = features.shape
    keys = bank.shape[0]
    cells = owners * banks // 2
    message = TILE + frames // banks * TILE
    block = min(owners * frames, 128)
    vmem = pl.BlockSpec(memory_space=pltpu.VMEM)
    loss, grad = pl.pallas_call(
        functools.partial(kernel, owners, banks, 3.0 * math.sqrt(width)),
        out_shape=(jax.ShapeDtypeStruct((1, frames), F32), jax.ShapeDtypeStruct((frames, width), F32)),
        in_specs=[pl.BlockSpec(memory_space=pltpu.HBM)] * 4,
        out_specs=(vmem, vmem),
        scratch_shapes=[
            pltpu.VMEM((frames, width), F32),
            pltpu.VMEM((1, frames), jnp.int32),
            pltpu.VMEM((1, frames), F32),
            pltpu.VMEM((keys, width), F32),
            pltpu.VMEM((keys, 3 * width), BF16),
            pltpu.VMEM((keys, 2 * width), BF16),
            pltpu.VMEM((2 * frames, width), F32),
            pltpu.VMEM((owners, 2 * frames, width), F32),
            pltpu.VMEM((block, keys), F32),
            pltpu.VMEM((block, keys), F32),
            pltpu.VMEM((2, cells, message, width), F32),
            pltpu.VMEM((cells, message, width), F32),
            pltpu.VMEM((cells, message, width), F32),
            pltpu.VMEM((frames + TILE, width), F32),
            pltpu.VMEM((banks, frames + TILE, width), F32),
            pltpu.SemaphoreType.DMA((4,)),
            pltpu.SemaphoreType.DMA((4,)),
            pltpu.SemaphoreType.DMA((4,)),
        ],
        compiler_params=pltpu.CompilerParams(
            collective_id=0, has_side_effects=True, vmem_limit_bytes=60 * 1024 * 1024),
    )(features, video_ids, bank, loss_weight.reshape(1, frames))
    return loss.reshape(frames), grad


def solution(mesh):
    return jax.shard_map(
        functools.partial(shards, mesh.shape["dp"], mesh.shape["bank"]),
        mesh=mesh,
        in_specs=(P("dp", None), P("dp", None), P(("dp", "bank"), None), P("dp")),
        out_specs=(P("dp"), P("dp", None)),
        check_vma=False,
    )
```

```python
import functools
import math

import jax
import jax.numpy as jnp
from jax import lax
from jax.experimental import pallas as pl
from jax.experimental.pallas import tpu as pltpu
from jax.sharding import PartitionSpec as P

EPSILON = 1e-06
TAU_BACK = 0.1
HIGHEST = lax.Precision.HIGHEST
MESH = pl.DeviceIdType.MESH
F32, BF16 = jnp.float32, jnp.bfloat16
TILE = 8
NT = (((1,), (1,)), ((), ()))
TN = (((0,), (0,)), ((), ()))
NN = (((1,), (0,)), ((), ()))


def split(values):
    high = values.astype(BF16)
    low = (values - high.astype(F32)).astype(BF16)
    return high, low


def inverse_lengths(values):
    return lax.rsqrt(jnp.sum(values * values, axis=1, keepdims=True) + EPSILON)


def cycle(near, normed, squares, same, pos_row, pos_col, weight):
    products = lax.dot_general(near, normed, NT, precision=HIGHEST, preferred_element_type=F32)
    norms = jnp.sum(near * near, axis=1, keepdims=True)
    distance = norms - 2.0 * products + squares
    back = jnp.where(same, jnp.exp(-distance / TAU_BACK), 0.0)
    beta = back / jnp.sum(back, axis=1, keepdims=True)
    mean = jnp.sum(beta * pos_row, axis=1, keepdims=True)
    square = jnp.sum(beta * (pos_row * pos_row), axis=1, keepdims=True)
    variance = square - mean * mean
    spread = jnp.maximum(variance, 1.0)
    off = pos_col - mean
    loss = off * off / spread + 0.5 * jnp.log(spread)
    d_spread = 0.5 / spread - off * off / (spread * spread)
    slope = jnp.where(variance > 1.0, 1.0, jnp.where(variance == 1.0, 0.5, 0.0))
    d_square = d_spread * slope
    d_mean = -2.0 * off / spread - 2.0 * mean * d_square
    d_beta = d_mean * pos_row + d_square * (pos_row * pos_row)
    d_logit = beta * (d_beta - (d_mean * mean + d_square * square))
    d_dist = d_logit * weight * (-1.0 / TAU_BACK)
    along = 2.0 * jnp.sum(d_dist * (norms - products), axis=1, keepdims=True)
    return loss, d_dist, along


def kernel(
    owners, banks, sharpness,
    feat_hbm, ids_hbm, bank_ref, weight_hbm,
    loss_ref, grad_ref,
    feat_ref, ids_ref, weight_ref, keys_buf, k3, kcat, out0, raw, score, expo,
    send1, recvx, recv1, tile4, recv4,
    load_sems, send_sems, recv_sems,
):
    frames, width = feat_hbm.shape
    share = frames // banks
    halves = banks // 2
    cells = owners * halves
    folds = frames // TILE
    block = min(owners * frames, 128)
    blocks = owners * frames // block
    group = block // frames
    pairs_rows = share * TILE
    sent = pairs_rows + share + 1
    lane_pick = lax.broadcasted_iota(jnp.int32, (share, width), 1) == lax.broadcasted_iota(jnp.int32, (share, width), 0)
    own = lax.axis_index("dp")
    part = lax.axis_index("bank")
    side = lax.rem(part, 2)
    twin = part + 1 - 2 * side
    cell = own * halves + lax.div(part, 2)

    loads = [
        pltpu.make_async_copy(feat_hbm, feat_ref, load_sems.at[0]),
        pltpu.make_async_copy(bank_ref, keys_buf, load_sems.at[1]),
        pltpu.make_async_copy(ids_hbm, ids_ref, load_sems.at[2]),
        pltpu.make_async_copy(weight_hbm, weight_ref, load_sems.at[3]),
    ]
    for load in loads:
        load.start()
    barrier = pltpu.get_barrier_semaphore()

    def every_cell(body):
        def step(k, carry):
            dst = lax.rem(cell + k, cells)
            body(dst, (lax.div(dst, halves), 2 * lax.rem(dst, halves) + side))
            return carry
        lax.fori_loop(1, cells, step, 0, unroll=cells <= 16)

    every_cell(lambda dst, where: pl.semaphore_signal(barrier, inc=1, device_id=where, device_id_type=MESH))
    for k in range(1, banks, 2):
        pl.semaphore_signal(barrier, inc=1, device_id=(own, lax.rem(part + k, banks)), device_id_type=MESH)

    for index in (0, 2, 3):
        loads[index].wait()
    features = feat_ref[...]
    inv_own = inverse_lengths(features)
    normed = features * inv_own
    ones = jnp.ones((TILE, width), F32)
    squares = lax.dot_general(ones, normed * normed, NT, precision=HIGHEST, preferred_element_type=F32)[0:1]
    ids = ids_ref[...].astype(F32)
    weights = weight_ref[...]

    def column(row, first, rows):
        pick = lax.broadcasted_iota(jnp.int32, (rows, frames), 1) == (
            lax.broadcasted_iota(jnp.int32, (rows, frames), 0) + first)
        return jnp.sum(jnp.where(pick, jnp.broadcast_to(row, (rows, frames)), 0.0), axis=1, keepdims=True)

    rows16 = lax.broadcasted_iota(jnp.int32, (frames, frames), 0)
    cols16 = lax.broadcasted_iota(jnp.int32, (frames, frames), 1)
    same_all = column(ids, 0, frames) == ids
    pos_row = jnp.sum(jnp.where(same_all & (rows16 < cols16), 1.0, 0.0), axis=0, keepdims=True)
    mine = part * share
    same_mine = column(ids, mine, share) == ids
    pos_mine = column(pos_row, mine, share)
    weight_mine = column(weights, mine, share)

    out0[0:frames, :] = features
    out0[frames:2 * frames, :] = jnp.zeros((frames, width), F32)
    out0[frames:2 * frames, 0:frames] = jnp.where(same_all, 1.0, 0.0)

    pl.semaphore_wait(barrier, cells - 1 + halves)

    def send_features(k, carry):
        dst = lax.rem(own + k, owners)
        pltpu.make_async_remote_copy(
            src_ref=out0, dst_ref=raw.at[own], send_sem=send_sems.at[0], recv_sem=recv_sems.at[0],
            device_id=(dst, part), device_id_type=MESH).start()
        return carry
    lax.fori_loop(1, owners, send_features, 0, unroll=owners <= 8)
    raw[own] = out0[...]

    loads[1].wait()
    bank = keys_buf[...]
    key_high, key_low = split(bank * inverse_lengths(bank))
    k3[:, 0:width] = key_high
    k3[:, width:2 * width] = key_high
    k3[:, 2 * width:3 * width] = key_low
    kcat[:, 0:width] = key_high
    kcat[:, width:2 * width] = key_low

    def wait(ref, sem):
        pltpu.make_async_copy(ref, ref, sem).wait()

    def project(values):
        high, low = split(values)
        joined = jnp.concatenate([high, low, high], axis=1)
        return lax.dot_general(joined, k3[...], NT, preferred_element_type=F32)

    def collect(values):
        high, low = split(values)
        both = lax.dot_general(high, kcat[...], NN, preferred_element_type=F32)
        rest = lax.dot_general(low, kcat[:, 0:width], NN, preferred_element_type=F32)
        return both[:, 0:width] + (both[:, width:2 * width] + rest)

    def each(count, body):
        if count <= 8:
            for k in range(count):
                body(k)
        else:
            lax.fori_loop(0, count, lambda k, carry: (body(k), carry)[1], 0)

    wait(raw.at[pl.ds(0, owners - 1)], recv_sems.at[0])

    def forward(index):
        queries = raw[pl.ds(index * group, group), 0:frames].reshape(block, width)
        scores = project(queries * inverse_lengths(queries))
        weighted = jnp.exp(sharpness * scores)
        score[...] = scores
        expo[...] = weighted
        summed = collect(weighted)
        partition = jnp.broadcast_to(jnp.sum(weighted, axis=1, keepdims=True), (block, width))
        for g in range(group):
            owner = index * group + g
            shared = raw[owner, frames:2 * frames, 0:frames]
            for b in range(banks):
                spot = send1.at[b % 2, owner * halves + b // 2]
                row = g * frames + b * share
                spot[pairs_rows:pairs_rows + share, :] = summed[row:row + share]
                spot[pairs_rows + share:sent, :] = jnp.sum(jnp.where(lane_pick, partition[row:row + share], 0.0), axis=0, keepdims=True)
            pairs = []
            for i in range(frames):
                picked = None
                for f in range(folds):
                    term = shared[f * TILE:(f + 1) * TILE, i:i + 1] * score[pl.ds(g * frames + f * TILE, TILE), :]
                    picked = term if picked is None else picked + term
                pairs.append(picked * expo[pl.ds(g * frames + i, 1), :])
            second = collect(jnp.concatenate(pairs, axis=0))
            for i in range(frames):
                b = i // share
                first = (i % share) * TILE
                send1[b % 2, owner * halves + b // 2, first:first + TILE, :] = second[i * TILE:(i + 1) * TILE]
    each(blocks, forward)

    pltpu.make_async_remote_copy(
        src_ref=send1.at[1 - side, :, 0:sent], dst_ref=recvx.at[:, 0:sent], send_sem=send_sems.at[1], recv_sem=recv_sems.at[1],
        device_id=(own, twin), device_id_type=MESH).start()
    wait(recvx.at[:, 0:sent], recv_sems.at[1])
    send1[side, :, 0:sent] = send1[side, :, 0:sent] + recvx[:, 0:sent]

    every_cell(lambda dst, where: pltpu.make_async_remote_copy(
        src_ref=send1.at[side, dst, 0:sent], dst_ref=recv1.at[cell, 0:sent], send_sem=send_sems.at[2], recv_sem=recv_sems.at[2],
        device_id=where, device_id_type=MESH).start())
    recv1[cell, 0:sent] = send1[side, cell, 0:sent]
    wait(recv1.at[pl.ds(0, cells - 1), 0:sent], recv_sems.at[2])
    total = jnp.sum(recv1[:, 0:sent], axis=0)
    parts = jnp.broadcast_to(total[pairs_rows + share:sent], (share, width))
    inv_part = 1.0 / jnp.sum(jnp.where(lane_pick, parts, 0.0), axis=1, keepdims=True)
    near = total[pairs_rows:pairs_rows + share] * inv_part
    loss, d_dist, along = cycle(near, normed, squares, same_mine, pos_row, pos_mine, weight_mine)
    pairs = share * TILE
    fold = jnp.where(
        lax.rem(lax.broadcasted_iota(jnp.int32, (frames, pairs), 0), TILE)
        == lax.rem(lax.broadcasted_iota(jnp.int32, (frames, pairs), 1), TILE), -2.0, 0.0)
    factors = lax.dot_general(d_dist, fold, NN, precision=HIGHEST, preferred_element_type=F32)
    factors = jnp.where(
        lax.div(lax.broadcasted_iota(jnp.int32, (share, pairs), 1), TILE)
        == lax.broadcasted_iota(jnp.int32, (share, pairs), 0), factors, 0.0)
    moment = lax.dot_general(factors, total[0:pairs], NN, precision=HIGHEST, preferred_element_type=F32)
    rows = sharpness * (moment * inv_part - along * near)
    joined = jnp.concatenate([near, jnp.ones((share, width), F32)], axis=1)
    local = lax.dot_general(d_dist, joined, TN, precision=HIGHEST, preferred_element_type=F32)
    local = 2.0 * (normed * local[:, width:2 * width] - local[:, 0:width])
    placed = jnp.concatenate([rows] * banks, axis=0)
    is_mine = lax.div(lax.broadcasted_iota(jnp.int32, (frames, width), 0), share) == part
    tile4[0:frames, :] = local + jnp.where(is_mine, placed, 0.0)
    tile4[frames:frames + TILE, :] = jnp.zeros((TILE, width), F32)
    tile4[frames:frames + share, :] = jnp.broadcast_to(loss, (share, width))

    for k in range(1, banks):
        pltpu.make_async_remote_copy(
            src_ref=tile4, dst_ref=recv4.at[part], send_sem=send_sems.at[3], recv_sem=recv_sems.at[3],
            device_id=(own, lax.rem(part + k, banks)), device_id_type=MESH).start()
    recv4[part] = tile4[...]
    wait(raw.at[pl.ds(0, owners - 1)], send_sems.at[0])
    wait(recvx.at[:, 0:sent], send_sems.at[1])
    wait(recv1.at[pl.ds(0, cells - 1), 0:sent], send_sems.at[2])
    wait(recv4.at[pl.ds(0, banks - 1)], recv_sems.at[3])
    held = recv4[...]
    grad_unit = jnp.sum(held[:, 0:frames], axis=0)
    grad_ref[...] = (grad_unit - normed * jnp.sum(normed * grad_unit, axis=1, keepdims=True)) * inv_own
    losses = jnp.concatenate([held[b, frames:frames + share] for b in range(banks)], axis=0)[:, 0:frames]
    loss_ref[...] = jnp.sum(jnp.where(rows16 == cols16, losses, 0.0), axis=0, keepdims=True)
    wait(recv4.at[pl.ds(0, banks - 1)], send_sems.at[3])


def shards(owners, banks, features, video_ids, bank, loss_weight):
    frames, width = features.shape
    keys = bank.shape[0]
    cells = owners * banks // 2
    message = TILE + frames // banks * TILE
    block = min(owners * frames, 128)
    vmem = pl.BlockSpec(memory_space=pltpu.VMEM)
    loss, grad = pl.pallas_call(
        functools.partial(kernel, owners, banks, 3.0 * math.sqrt(width)),
        out_shape=(jax.ShapeDtypeStruct((1, frames), F32), jax.ShapeDtypeStruct((frames, width), F32)),
        in_specs=[pl.BlockSpec(memory_space=pltpu.HBM)] * 4,
        out_specs=(vmem, vmem),
        scratch_shapes=[
            pltpu.VMEM((frames, width), F32),
            pltpu.VMEM((1, frames), jnp.int32),
            pltpu.VMEM((1, frames), F32),
            pltpu.VMEM((keys, width), F32),
            pltpu.VMEM((keys, 3 * width), BF16),
            pltpu.VMEM((keys, 2 * width), BF16),
            pltpu.VMEM((2 * frames, width), F32),
            pltpu.VMEM((owners, 2 * frames, width), F32),
            pltpu.VMEM((block, keys), F32),
            pltpu.VMEM((block, keys), F32),
            pltpu.VMEM((2, cells, message, width), F32),
            pltpu.VMEM((cells, message, width), F32),
            pltpu.VMEM((cells, message, width), F32),
            pltpu.VMEM((frames + TILE, width), F32),
            pltpu.VMEM((banks, frames + TILE, width), F32),
            pltpu.SemaphoreType.DMA((4,)),
            pltpu.SemaphoreType.DMA((4,)),
            pltpu.SemaphoreType.DMA((4,)),
        ],
        compiler_params=pltpu.CompilerParams(
            collective_id=0, has_side_effects=True, vmem_limit_bytes=60 * 1024 * 1024),
    )(features, video_ids, bank, loss_weight.reshape(1, frames))
    return loss.reshape(frames), grad


def solution(mesh):
    return jax.shard_map(
        functools.partial(shards, mesh.shape["dp"], mesh.shape["bank"]),
        mesh=mesh,
        in_specs=(P("dp", None), P("dp", None), P(("dp", "bank"), None), P("dp")),
        out_specs=(P("dp"), P("dp", None)),
        check_vma=False,
    )
```
